32 devices in a mesh: leaf: 32 (over z, y, x, core).
Axes of the slice: x: 2, y: 2, z: 4, core: 2. Of those that a mesh axis runs over, the one named last changes fastest.
Arguments:
- points: bfloat16 [32768, 512], P('leaf'), may hold values from -6 to 6
- weights: float32 [32768, 64], P('leaf'), may hold values from -6 to 6
- leaf_basis: float32 [32768, 256], P('leaf'), may hold values from -0.1875 to 0.1875
- transfer: float32 [32, 4, 256, 256], P('leaf'), may hold values from -0.375 to 0.375
- skeleton_index: int32 [5, 32, 256], replicated, may hold values from 0 to 1023, as said below
- node_owner: int32 [3, 32], replicated, may hold values from 0 to 7, as said below
- near_list: int32 [32, 3], replicated, may hold values from 0 to 7, as said below
Outputs:
- product: float32 [32768, 64], P('leaf')
The draws below stay inside these ranges and needn't reach their ends.
Inputs may be any that keep to these rules, and one draw needn't show every extreme that they name: `near_list`: entry m > 0 of row i names leaf i XOR m of the same aligned group of 8 leaves; 0 marks an empty slot. The nonzero entries of a row are distinct and number 1 to 3; some row has 3. `skeleton_index`: row 0, column i: 256 distinct row numbers below 1024 within leaf i. Row m >= 1, column s below 32 >> m: 256 distinct row numbers below 512; other columns are unused. `node_owner`: row m - 1, column s below 32 >> m: a number below 2 to the power m; other columns are unused.
All inputs are finite; a program needn't handle non-finite values.
Results may differ from the reference program's by a relative error of at most 0.0018.
Values may be sent and summed in bfloat16 or wider, within the bound.
A program may use at most 128 MiB of HBM per device.

```python
import jax
import jax.numpy as jnp
from jax import lax

LEAF_PTS = 1024
EMBED = 512
RANK = 256
RHS = 64
GROUP = 8
NEAR_MAX = 3
LEVELS = 5
TOTAL_PTS = 32768
N_LEAF = 32


def draw_skeleton_index(key, part):
    subkeys = jax.random.split(key, LEVELS * N_LEAF)
    leaf_rows = jax.vmap(lambda subkey: jax.random.permutation(subkey, LEAF_PTS)[:RANK])(subkeys[:N_LEAF])
    node_rows = jax.vmap(lambda subkey: jax.random.permutation(subkey, 2 * RANK)[:RANK])(subkeys[N_LEAF:])
    return jnp.concatenate([leaf_rows[None], node_rows.reshape(LEVELS - 1, N_LEAF, RANK)], 0).astype(jnp.int32)


def draw_node_owner(key, part):
    heights = jnp.arange(1, LEVELS - 1, dtype=jnp.int32)
    limits = jnp.left_shift(jnp.ones_like(heights), heights)[:, None]
    raw_values = jax.random.randint(key, (LEVELS - 2, N_LEAF), 0, 1 << 30)
    return (raw_values % limits).astype(jnp.int32)


def draw_near_list(key, part):
    order_key, count_key, heavy_key = jax.random.split(key, 3)
    orders = jax.vmap(lambda subkey: jax.random.permutation(subkey, GROUP - 1) + 1)(jax.random.split(order_key, N_LEAF))
    raw_counts = jax.random.randint(count_key, (N_LEAF,), 0, 20)
    counts = 1 + (raw_counts >= 12).astype(jnp.int32) + (raw_counts >= 17).astype(jnp.int32)
    heavy_leaf = jax.random.randint(heavy_key, (), 0, N_LEAF)
    counts = counts.at[heavy_leaf].set(NEAR_MAX)
    near_slots = jnp.arange(NEAR_MAX, dtype=jnp.int32)
    return jnp.where(near_slots[None, :] < counts[:, None], orders[:, :NEAR_MAX], 0).astype(jnp.int32)


def block_scale(stream_key, dims, shards, least, top_value):
    gain = 1.0
    for dim, parts in shards:
        steps = jax.random.uniform(jax.random.fold_in(jax.random.fold_in(stream_key, 6), dim), (parts,), jnp.float32, least / len(shards), top_value / len(shards))
        gain = gain * jnp.repeat(jnp.exp(steps), dims[dim] // parts).reshape((-1,) + (1,) * (len(dims) - 1 - dim))
    return gain


def scatter_about(own_key, extent, width, bound, cuts=(), kind=jnp.bfloat16):
    level = block_scale(own_key, extent, cuts, -0.22, 0.18) if cuts else 1.0
    entries = jax.random.normal(own_key, extent, jnp.float32) * width * level
    return jnp.minimum(jnp.maximum(entries, -bound), bound).astype(kind)


def setup_inputs(seed: int = 0) -> dict:
    seeds = jax.random.split(jax.random.key(seed), 8)
    return {
        "points": scatter_about(seeds[0], (TOTAL_PTS, EMBED), 1.0, 6.0, ((0, 32),)),
        "weights": scatter_about(seeds[1], (TOTAL_PTS, RHS), 1.0, 6.0, ((0, 32),), jnp.float32),
        "leaf_basis": scatter_about(seeds[2], (TOTAL_PTS, RANK), LEAF_PTS ** -0.5, 0.1875, ((0, 32),), jnp.float32),
        "transfer": scatter_about(seeds[3], (N_LEAF, LEVELS - 1, RANK, RANK), RANK ** -0.5, 0.375, ((0, 32),), jnp.float32),
        "skeleton_index": draw_skeleton_index(jax.random.fold_in(seeds[7], 71), 0),
        "node_owner": draw_node_owner(jax.random.fold_in(seeds[7], 71), 0),
        "near_list": draw_near_list(jax.random.fold_in(seeds[7], 71), 0),
    }


PRECISE = lax.Precision.HIGHEST


def kernel_block(left_rows, right_rows):
    scale_factor = 2.0 / left_rows.shape[1]
    left_norm = jnp.sum(jnp.square(left_rows.astype(jnp.float32)), axis=1)
    right_norm = jnp.sum(jnp.square(right_rows.astype(jnp.float32)), axis=1)
    inner_products = lax.dot_general(left_rows, right_rows, (((1,), (1,)), ((), ())), preferred_element_type=jnp.float32)
    return jnp.exp(-scale_factor * (left_norm[:, None] + right_norm[None, :] - 2.0 * inner_products))


def apply_matrix(matrix, values):
    return jnp.dot(matrix, values, precision=PRECISE, preferred_element_type=jnp.float32)


def pick_rows(blocks, picks):
    return jax.vmap(lambda block_rows, row_picks: jnp.take(block_rows, row_picks, axis=0))(blocks, picks)


def owner_of(height, node_count, node_owner):
    node_ids = jnp.arange(node_count, dtype=jnp.int32) * (1 << height)
    if height == 0:
        return node_ids
    return node_ids + node_owner[height - 1, :node_count]


def reference(points, weights, leaf_basis, transfer, skeleton_index, node_owner, near_list):
    leaf_points = points.reshape(N_LEAF, LEAF_PTS, EMBED)
    leaf_weights = weights.reshape(N_LEAF, LEAF_PTS, RHS)
    leaf_bases = leaf_basis.reshape(N_LEAF, LEAF_PTS, RANK)
    leaf_ids = jnp.arange(N_LEAF, dtype=jnp.int32)

    def near_leaf(leaf_number):
        own_points = leaf_points[leaf_number]
        running_sum = apply_matrix(kernel_block(own_points, own_points), leaf_weights[leaf_number])
        for near_slot in range(NEAR_MAX):
            offset = near_list[leaf_number, near_slot]
            partner = jnp.bitwise_xor(leaf_number, offset)
            near_term = apply_matrix(kernel_block(own_points, leaf_points[partner]), leaf_weights[partner])
            running_sum = running_sum + jnp.where(offset > 0, near_term, 0.0)
        return running_sum

    near_part = lax.map(near_leaf, leaf_ids)

    node_coeff = jnp.einsum("nlk,nlr->nkr", leaf_bases, leaf_weights, precision=PRECISE)
    node_rows = pick_rows(leaf_points, skeleton_index[0])
    level_coeff = []
    level_rows = []
    for height in range(LEVELS):
        level_coeff.append(node_coeff)
        level_rows.append(node_rows)
        if height + 1 < LEVELS:
            node_count = N_LEAF >> height
            transfer_stack = transfer[owner_of(height, node_count, node_owner), height]
            lifted = jnp.einsum("nkj,nkr->njr", transfer_stack, node_coeff, precision=PRECISE)
            node_coeff = lifted[0::2] + lifted[1::2]
            joined = jnp.concatenate([node_rows[0::2], node_rows[1::2]], axis=1)
            node_rows = pick_rows(joined, skeleton_index[height + 1, : node_count // 2])

    def sibling_coupling(height):
        rows_here = level_rows[height]
        coeff_here = level_coeff[height]
        sibling = jnp.bitwise_xor(jnp.arange(rows_here.shape[0], dtype=jnp.int32), 1)
        blocks = jax.vmap(kernel_block)(rows_here, rows_here[sibling])
        return jnp.einsum("nkj,njr->nkr", blocks, coeff_here[sibling], precision=PRECISE)

    down_field = sibling_coupling(LEVELS - 1)
    for height in range(LEVELS - 2, -1, -1):
        node_count = N_LEAF >> height
        transfer_stack = transfer[owner_of(height, node_count, node_owner), height]
        down_field = jnp.einsum("nkj,njr->nkr", transfer_stack, jnp.repeat(down_field, 2, axis=0), precision=PRECISE)
        if height >= 3:
            down_field = down_field + sibling_coupling(height)

    def far_leaf(leaf_number):
        own_rows = level_rows[0][leaf_number]
        group_start = leaf_number - leaf_number % GROUP
        running_sum = jnp.zeros((RANK, RHS), jnp.float32)
        for target in range(GROUP):
            partner = group_start + target
            offset = jnp.bitwise_xor(leaf_number, partner)
            distant = (offset != 0) & jnp.logical_not(jnp.any(near_list[leaf_number] == offset))
            far_term = apply_matrix(kernel_block(own_rows, level_rows[0][partner]), level_coeff[0][partner])
            running_sum = running_sum + jnp.where(distant, far_term, 0.0)
        return running_sum

    down_field = down_field + lax.map(far_leaf, leaf_ids)
    far_part = jnp.einsum("nlk,nkr->nlr", leaf_bases, down_field, precision=PRECISE)
    return (near_part + far_part).reshape(N_LEAF * LEAF_PTS, RHS)
```

```python
import functools

import jax
import jax.numpy as jnp
from jax import lax
from jax.experimental import pallas as pl
from jax.experimental.pallas import tpu as pltpu
from jax.sharding import PartitionSpec as P

MESH = pl.DeviceIdType.MESH
GROUP = 8
CHUNKS = 4
TOP = 3
F32 = jnp.float32
BF16 = jnp.bfloat16
PRECISE = lax.Precision.HIGHEST


def split(value):
    high = value.astype(BF16)
    return high, (value - high.astype(F32)).astype(BF16)


def mm(left, right, precision=None):
    return jnp.dot(left, right, precision=precision, preferred_element_type=F32)


def mm_nt(left, right, precision=None):
    return lax.dot_general(
        left, right, (((1,), (1,)), ((), ())), precision=precision, preferred_element_type=F32
    )


def as_row(column):
    return jnp.broadcast_to(column, (column.shape[0], 128)).T[:1]


def as_column(row):
    return jnp.broadcast_to(row, (128, row.shape[1])).T[:, :1]


def norm_column(rows, scale):
    wide = rows.astype(F32)
    return -scale * jnp.sum(wide * wide, axis=1, keepdims=True)


def gauss(left, left_norm, right, right_norm, scale):
    return jnp.exp((2.0 * scale) * mm_nt(left, right) + (left_norm + right_norm))


def contract(coeff, block):
    high, low = split(block)
    return mm(coeff, high) + mm(coeff, low)


def contract_both(coeff_high, coeff_low, block):
    high, low = split(block)
    both = mm(jnp.concatenate([coeff_high, coeff_low], 0), high)
    count = coeff_high.shape[0]
    return both[:count] + both[count:] + mm(coeff_high, low)


def put_folded(ref, row, value):
    half, width = value.shape[0] // 2, value.shape[1]
    ref[row : row + half, :width] = value[:half]
    ref[row : row + half, width:] = value[half:]


def get_folded(ref, row, height, width):
    half = height // 2
    return jnp.concatenate([ref[row : row + half, :width], ref[row : row + half, width:]], 0)


def message_rows(levels, rank, rhs, height):
    rows = {"Z": 0}
    at = rank
    if height >= TOP:
        rows["w"] = at
        at += rhs
    if height + 1 < levels:
        rows["p"] = at
        at += rhs
    for upper in range(height + 1, levels - 1):
        rows[upper] = at
        at += rank
    return rows, at


def kernel(levels, scale, tile, *refs):
    x_ref, b_ref, v_ref, t_ref, skel_ref, owner_ref, near_ref, out_ref = refs[:8]
    G, acc, far_acc, norm_row = refs[8:12]
    sent = refs[12 : 12 + levels]
    came = refs[12 + levels : 12 + 2 * levels]
    bulk_send, bulk_recv, tree_send, tree_recv, relay_send, relay_recv = refs[12 + 2 * levels :]
    me = lax.axis_index("leaf")
    points, embed = x_ref.shape
    rhs, rank = b_ref.shape[1], v_ref.shape[1]
    rows_each = points // CHUNKS
    pitch = rows_each + rhs
    tail = CHUNKS * pitch

    def partner(mask):
        where = me
        for bit in range(levels):
            if mask >> bit & 1:
                where = where + (1 << bit) * (1 - 2 * ((me // (1 << bit)) % 2))
        return where

    core = me % 2

    def picks(level, node):
        return as_column(skel_ref[level, pl.ds(node, 1), :])

    def one_hot(column, width, base):
        lane = lax.broadcasted_iota(jnp.int32, (column.shape[0], width), 1) + base
        return jnp.where(lane == column, 1.0, 0.0).astype(BF16)

    near_ids = [near_ref[me, slot] for slot in range(near_ref.shape[1])]

    def near_flag(offset):
        hit = near_ids[0] == offset
        for other in near_ids[1:]:
            hit = hit | (other == offset)
        return jnp.where(hit, 1.0, 0.0)

    b_t = jnp.concatenate([b_ref[...], jnp.zeros_like(b_ref)], 1).T[:rhs]
    b_high, b_low = split(b_t)
    for q in range(CHUNKS):
        G[0, q * pitch : q * pitch + rows_each, :] = x_ref[q * rows_each : (q + 1) * rows_each, :]
        put_folded(G.at[0], q * pitch + rows_each, b_high[:, q * rows_each : (q + 1) * rows_each])
        put_folded(
            G.at[0], q * pitch + rows_each + rhs // 2, b_low[:, q * rows_each : (q + 1) * rows_each]
        )
    w = mm(b_t, v_ref[...], PRECISE)
    w_high, w_low = split(w)
    put_folded(G.at[0], tail, w_high)
    norm_row[...] = as_row(norm_column(x_ref[...], scale))
    pick = picks(0, me)
    Z = mm(one_hot(pick, points, 0), x_ref[...]).astype(BF16)
    leaf_Z = Z
    leaf_Z_row = as_row(norm_column(Z, scale))
    lifts = {}
    for height in range(1, levels - 1):
        mine = me % (1 << height) == owner_ref[height - 1, me // (1 << height)]
        lifts[height] = t_ref[0, height] * jnp.where(mine, 1.0, 0.0)

    layouts = [message_rows(levels, rank, rhs, height) for height in range(levels)]

    def write_message(height, w, Z, partial, lifts):
        rows, _ = layouts[height]
        buf = sent[height]
        buf[0:rank, :] = Z
        for key, value in (("w", w), ("p", partial)):
            if key in rows:
                high, low = split(value)
                put_folded(buf, rows[key], high)
                put_folded(buf, rows[key] + rhs // 2, low)
        for upper in range(height + 1, levels - 1):
            high, low = split(lifts[upper])
            put_folded(buf, rows[upper], high)
            put_folded(buf, rows[upper] + rank // 2, low)

    def read_pair(height, key):
        row = layouts[height][0][key]
        high = get_folded(came[height], row, rhs, rank)
        low = get_folded(came[height], row + rhs // 2, rhs, rank)
        return high, low

    def tree_copy(height):
        size = layouts[height][1]
        if height == 0:
            part = pl.ds(0, size)
        else:
            part = pl.ds(pl.multiple_of(core * (size // 2), 16), size // 2)
        return pltpu.make_async_remote_copy(
            src_ref=sent[height].at[part],
            dst_ref=came[height].at[part],
            send_sem=tree_send.at[height],
            recv_sem=tree_recv.at[height],
            device_id=(partner(1 << height),),
            device_id_type=MESH,
        )

    def relay_copy(height):
        size = layouts[height][1]
        part = pl.ds(pl.multiple_of(core * (size // 2), 16), size // 2)
        return pltpu.make_async_remote_copy(
            src_ref=came[height].at[part],
            dst_ref=came[height].at[part],
            send_sem=relay_send.at[height],
            recv_sem=relay_recv.at[height],
            device_id=(partner(1),),
            device_id_type=MESH,
        )

    def relay_wait(height):
        size = layouts[height][1]
        part = pl.ds(pl.multiple_of((1 - core) * (size // 2), 16), size // 2)
        pltpu.make_async_remote_copy(
            src_ref=came[height].at[part],
            dst_ref=came[height].at[part],
            send_sem=relay_send.at[height],
            recv_sem=relay_recv.at[height],
            device_id=(partner(1),),
            device_id_type=MESH,
        ).wait_recv()

    routes = {1: (0, 1), 2: (0, 2), 4: (0, 4), 3: (2, 1), 5: (4, 1), 7: (6, 1)}

    def bulk(slot, q):
        if slot == 6:
            source, mask = (2, 4) if q < CHUNKS // 2 else (4, 2)
        else:
            source, mask = routes[slot]
        extent = pitch + (rhs // 2 if q == CHUNKS - 1 else 0)
        part = pl.ds(q * pitch, extent)
        return pltpu.make_async_remote_copy(
            src_ref=G.at[source, part],
            dst_ref=G.at[slot, part],
            send_sem=bulk_send.at[slot, q],
            recv_sem=bulk_recv.at[slot, q],
            device_id=(partner(mask),),
            device_id_type=MESH,
        )

    state = {}

    def lift(height, w):
        return mm(w, lifts[height] if height else t_ref[0, 0], PRECISE)

    state["w"], state["Z"], state["C"] = w, Z, {}
    state["partial"] = lift(0, w)
    write_message(0, w, Z, state["partial"], lifts)

    barrier = pltpu.get_barrier_semaphore()
    for bit in range(levels):
        pl.semaphore_signal(barrier, inc=1, device_id=(partner(1 << bit),), device_id_type=MESH)
    pl.semaphore_wait(barrier, levels)

    tree_copy(0).start()
    low_half, high_half = range(CHUNKS // 2), range(CHUNKS // 2, CHUNKS)
    for q, r in zip(low_half, high_half):
        bulk(2, q).start()
        bulk(4, r).start()
    for q in range(CHUNKS):
        bulk(1, q).start()

    acc[...] = jnp.zeros_like(acc)
    far_acc[...] = jnp.zeros_like(far_acc)
    for q in range(CHUNKS):
        own = x_ref[q * rows_each : (q + 1) * rows_each, :]
        own_norm = norm_column(own, scale)
        part = slice(q * rows_each, (q + 1) * rows_each)

        def own_tile(step, carry, own=own, own_norm=own_norm, part=part):
            at = pl.ds(pl.multiple_of(step * tile, tile), tile)
            block = gauss(own, own_norm, x_ref[at, :], norm_row[:, at], scale)
            acc[:, at] += contract_both(b_high[:, part], b_low[:, part], block)
            return carry

        lax.fori_loop(0, points // tile, own_tile, 0)

    def advance(height):
        rows = layouts[height][0]
        sibling_Z = came[height][0:rank, :]
        if height >= TOP:
            high, low = read_pair(height, "w")
            block = gauss(
                sibling_Z,
                norm_column(sibling_Z, scale),
                state["Z"],
                as_row(norm_column(state["Z"], scale)),
                scale,
            )
            state["C"][height] = contract_both(high, low, block)
        if height + 1 == levels:
            return
        high, low = read_pair(height, "p")
        state["w"] = state["partial"] + (high.astype(F32) + low.astype(F32))
        for upper in range(height + 1, levels - 1):
            high = get_folded(came[height], rows[upper], rank, rank)
            low = get_folded(came[height], rows[upper] + rank // 2, rank, rank)
            lifts[upper] = lifts[upper] + (high.astype(F32) + low.astype(F32))
        pick = picks(height + 1, me // (2 << height))
        shift = rank * ((me // (1 << height)) % 2)
        pick = jnp.where(pick >= shift, pick - shift, pick + shift)
        state["Z"] = (
            mm(one_hot(pick, rank, 0), state["Z"]) + mm(one_hot(pick, rank, rank), sibling_Z)
        ).astype(BF16)
        if height + 2 < levels:
            state["partial"] = lift(height + 1, state["w"])
        else:
            state["partial"] = None
        write_message(height + 1, state["w"], state["Z"], state["partial"], lifts)
        tree_copy(height + 1).start()

    tree_copy(0).wait_recv()
    advance(0)
    for q, r in zip(low_half, high_half):
        bulk(2, r).start()
        bulk(4, q).start()

    def arrive(slot, q):
        bulk(slot, q).wait_recv()
        if slot in (2, 4, 6):
            bulk(slot + 1, q).start()
        if (slot == 2 and q < CHUNKS // 2) or (slot == 4 and q >= CHUNKS // 2):
            bulk(6, q).start()

    def near(slot, q):
        at_row = q * pitch
        theirs = G[slot, at_row : at_row + rows_each, :]
        flag = near_flag(slot)
        high = get_folded(G.at[slot], at_row + rows_each, rhs, rows_each)
        low = get_folded(G.at[slot], at_row + rows_each + rhs // 2, rhs, rows_each)
        high = (high.astype(F32) * flag).astype(BF16)
        low = (low.astype(F32) * flag).astype(BF16)
        their_norm = norm_column(theirs, scale)

        def one_tile(step, carry):
            at = pl.ds(pl.multiple_of(step * tile, tile), tile)
            block = gauss(theirs, their_norm, x_ref[at, :], norm_row[:, at], scale)
            acc[:, at] += contract_both(high, low, block)
            return carry

        lax.fori_loop(0, points // tile, one_tile, 0)

    def far(slot):
        pick = picks(0, partner(slot))
        rows = None
        for q in range(CHUNKS):
            term = mm(
                one_hot(pick, rows_each, q * rows_each),
                G[slot, q * pitch : q * pitch + rows_each, :],
            )
            rows = term if rows is None else rows + term
        rows = rows.astype(BF16)
        coeff = get_folded(G.at[slot], tail, rhs, rank)
        coeff = (coeff.astype(F32) * (1.0 - near_flag(slot))).astype(BF16)
        block = gauss(rows, norm_column(rows, scale), leaf_Z, leaf_Z_row, scale)
        far_acc[...] += contract(coeff, block)

    def first_half(height):
        tree_copy(height).wait_recv()
        relay_copy(height).start()

    def second_half(height):
        relay_wait(height)
        advance(height)

    tree_steps = []
    for height in range(1, levels):
        tree_steps.append(functools.partial(first_half, height))
        tree_steps.append(functools.partial(second_half, height))

    def tree_step():
        if tree_steps:
            tree_steps.pop(0)()

    for q in range(CHUNKS):
        arrive(1, q)
        near(1, q)
    far(1)
    orders = [(q, r) for q, r in zip(low_half, high_half)]
    orders += [(r, q) for q, r in zip(low_half, high_half)]
    for q, r in orders:
        arrive(2, q)
        arrive(4, r)
        near(2, q)
        tree_step()
        near(4, r)
        arrive(3, q)
        arrive(5, r)
        near(3, q)
        tree_step()
        near(5, r)
    for slot in (2, 4, 3, 5):
        far(slot)
        tree_step()
    for q, r in zip(low_half, high_half):
        arrive(6, q)
        arrive(6, r)
        near(6, q)
        near(6, r)
    while tree_steps:
        tree_step()

    down = state["C"][levels - 1]
    for height in range(levels - 2, -1, -1):
        down = mm_nt(down, lifts[height] if height else t_ref[0, 0], PRECISE)
        if height in state["C"]:
            down = down + state["C"][height]
    for q in range(CHUNKS):
        arrive(7, q)
        near(7, q)
    far(6)
    far(7)
    total = acc[...] + mm_nt(down + far_acc[...], v_ref[...], PRECISE)
    out_ref[...] = jnp.concatenate([total, jnp.zeros_like(total)], 0).T[:, :rhs]

    for slot in range(1, GROUP):
        for q in range(CHUNKS):
            bulk(slot, q).wait_send()
    for height in range(levels):
        tree_copy(height).wait_send()
        if height:
            relay_copy(height).wait_send()


def solution(mesh):
    leaves = mesh.shape["leaf"]
    levels = leaves.bit_length() - 1

    def per_device(points, weights, leaf_basis, transfer, skeleton_index, node_owner, near_list):
        count, embed = points.shape
        rhs, rank = weights.shape[1], leaf_basis.shape[1]
        pitch = count // CHUNKS + rhs
        vmem = pl.BlockSpec(memory_space=pltpu.VMEM)
        smem = pl.BlockSpec(memory_space=pltpu.SMEM)
        sizes = [message_rows(levels, rank, rhs, height)[1] for height in range(levels)]
        buffers = [pltpu.VMEM((size, embed), BF16) for size in sizes]
        return pl.pallas_call(
            functools.partial(kernel, levels, 2.0 / embed, min(512, count)),
            out_shape=jax.ShapeDtypeStruct((count, rhs), F32),
            in_specs=[vmem] * 5 + [smem] * 2,
            out_specs=vmem,
            scratch_shapes=[
                pltpu.VMEM((GROUP, CHUNKS * pitch + rhs // 2, embed), BF16),
                pltpu.VMEM((rhs, count), F32),
                pltpu.VMEM((rhs, rank), F32),
                pltpu.VMEM((1, count), F32),
                *buffers,
                *buffers,
                pltpu.SemaphoreType.DMA((GROUP, CHUNKS)),
                pltpu.SemaphoreType.DMA((GROUP, CHUNKS)),
                pltpu.SemaphoreType.DMA((levels,)),
                pltpu.SemaphoreType.DMA((levels,)),
                pltpu.SemaphoreType.DMA((levels,)),
                pltpu.SemaphoreType.DMA((levels,)),
            ],
            compiler_params=pltpu.CompilerParams(
                collective_id=0, has_side_effects=True, vmem_limit_bytes=52 * 2**20
            ),
        )(points, weights, leaf_basis, transfer, skeleton_index, node_owner, near_list)

    return jax.shard_map(
        per_device,
        mesh=mesh,
        in_specs=(
            P("leaf", None),
            P("leaf", None),
            P("leaf", None),
            P("leaf", None, None, None),
            P(),
            P(),
            P(),
        ),
        out_specs=P("leaf", None),
        check_vma=False,
    )
```

```python
import functools

import jax
import jax.numpy as jnp
from jax import lax
from jax.experimental import pallas as pl
from jax.experimental.pallas import tpu as pltpu
from jax.sharding import PartitionSpec as P

MESH = pl.DeviceIdType.MESH
GROUP = 8
CHUNKS = 4
TOP = 3
F32 = jnp.float32
BF16 = jnp.bfloat16
PRECISE = lax.Precision.HIGHEST


def split(value):
    high = value.astype(BF16)
    return high, (value - high.astype(F32)).astype(BF16)


def mm(left, right, precision=None):
    return jnp.dot(left, right, precision=precision, preferred_element_type=F32)


def mm_nt(left, right, precision=None):
    return lax.dot_general(
        left, right, (((1,), (1,)), ((), ())), precision=precision, preferred_element_type=F32
    )


def as_row(column):
    return jnp.broadcast_to(column, (column.shape[0], 128)).T[:1]


def as_column(row):
    return jnp.broadcast_to(row, (128, row.shape[1])).T[:, :1]


def norm_column(rows, scale):
    wide = rows.astype(F32)
    return -scale * jnp.sum(wide * wide, axis=1, keepdims=True)


def gauss(left, left_norm, right, right_norm, scale):
    return jnp.exp((2.0 * scale) * mm_nt(left, right) + (left_norm + right_norm))


def contract(coeff, block):
    high, low = split(block)
    return mm(coeff, high) + mm(coeff, low)


def contract_both(coeff_high, coeff_low, block):
    high, low = split(block)
    both = mm(jnp.concatenate([coeff_high, coeff_low], 0), high)
    count = coeff_high.shape[0]
    return both[:count] + both[count:] + mm(coeff_high, low)


def put_folded(ref, row, value):
    half, width = value.shape[0] // 2, value.shape[1]
    ref[row : row + half, :width] = value[:half]
    ref[row : row + half, width:] = value[half:]


def get_folded(ref, row, height, width):
    half = height // 2
    return jnp.concatenate([ref[row : row + half, :width], ref[row : row + half, width:]], 0)


def message_rows(levels, rank, rhs, height):
    rows = {"Z": 0}
    at = rank
    if height >= TOP:
        rows["w"] = at
        at += rhs
    if height + 1 < levels:
        rows["p"] = at
        at += rhs
    for upper in range(height + 1, levels - 1):
        rows[upper] = at
        at += rank
    return rows, at


def kernel(levels, scale, tile, *refs):
    x_ref, b_ref, v_ref, t_ref, skel_ref, owner_ref, near_ref, out_ref = refs[:8]
    G, acc, far_acc, norm_row = refs[8:12]
    sent = refs[12 : 12 + levels]
    came = refs[12 + levels : 12 + 2 * levels]
    bulk_send, bulk_recv, tree_send, tree_recv, relay_send, relay_recv = refs[12 + 2 * levels :]
    me = lax.axis_index("leaf")
    points, embed = x_ref.shape
    rhs, rank = b_ref.shape[1], v_ref.shape[1]
    rows_each = points // CHUNKS
    pitch = rows_each + rhs
    tail = CHUNKS * pitch

    def partner(mask):
        where = me
        for bit in range(levels):
            if mask >> bit & 1:
                where = where + (1 << bit) * (1 - 2 * ((me // (1 << bit)) % 2))
        return where

    core = me % 2

    def picks(level, node):
        return as_column(skel_ref[level, pl.ds(node, 1), :])

    def one_hot(column, width, base):
        lane = lax.broadcasted_iota(jnp.int32, (column.shape[0], width), 1) + base
        return jnp.where(lane == column, 1.0, 0.0).astype(BF16)

    near_ids = [near_ref[me, slot] for slot in range(near_ref.shape[1])]

    def near_flag(offset):
        hit = near_ids[0] == offset
        for other in near_ids[1:]:
            hit = hit | (other == offset)
        return jnp.where(hit, 1.0, 0.0)

    b_t = jnp.concatenate([b_ref[...], jnp.zeros_like(b_ref)], 1).T[:rhs]
    b_high, b_low = split(b_t)
    for q in range(CHUNKS):
        G[0, q * pitch : q * pitch + rows_each, :] = x_ref[q * rows_each : (q + 1) * rows_each, :]
        put_folded(G.at[0], q * pitch + rows_each, b_high[:, q * rows_each : (q + 1) * rows_each])
        put_folded(
            G.at[0], q * pitch + rows_each + rhs // 2, b_low[:, q * rows_each : (q + 1) * rows_each]
        )
    w = mm(b_t, v_ref[...], PRECISE)
    w_high, w_low = split(w)
    put_folded(G.at[0], tail, w_high)
    norm_row[...] = as_row(norm_column(x_ref[...], scale))
    pick = picks(0, me)
    Z = mm(one_hot(pick, points, 0), x_ref[...]).astype(BF16)
    leaf_Z = Z
    leaf_Z_row = as_row(norm_column(Z, scale))
    lifts = {}
    for height in range(1, levels - 1):
        mine = me % (1 << height) == owner_ref[height - 1, me // (1 << height)]
        lifts[height] = t_ref[0, height] * jnp.where(mine, 1.0, 0.0)

    layouts = [message_rows(levels, rank, rhs, height) for height in range(levels)]

    def write_message(height, w, Z, partial, lifts):
        rows, _ = layouts[height]
        buf = sent[height]
        buf[0:rank, :] = Z
        for key, value in (("w", w), ("p", partial)):
            if key in rows:
                high, low = split(value)
                put_folded(buf, rows[key], high)
                put_folded(buf, rows[key] + rhs // 2, low)
        for upper in range(height + 1, levels - 1):
            high, low = split(lifts[upper])
            put_folded(buf, rows[upper], high)
            put_folded(buf, rows[upper] + rank // 2, low)

    def read_pair(height, key):
        row = layouts[height][0][key]
        high = get_folded(came[height], row, rhs, rank)
        low = get_folded(came[height], row + rhs // 2, rhs, rank)
        return high, low

    def tree_copy(height):
        size = layouts[height][1]
        if height == 0:
            part = pl.ds(0, size)
        else:
            part = pl.ds(pl.multiple_of(core * (size // 2), 16), size // 2)
        return pltpu.make_async_remote_copy(
            src_ref=sent[height].at[part],
            dst_ref=came[height].at[part],
            send_sem=tree_send.at[height],
            recv_sem=tree_recv.at[height],
            device_id=(partner(1 << height),),
            device_id_type=MESH,
        )

    def relay_copy(height):
        size = layouts[height][1]
        part = pl.ds(pl.multiple_of(core * (size // 2), 16), size // 2)
        return pltpu.make_async_remote_copy(
            src_ref=came[height].at[part],
            dst_ref=came[height].at[part],
            send_sem=relay_send.at[height],
            recv_sem=relay_recv.at[height],
            device_id=(partner(1),),
            device_id_type=MESH,
        )

    def relay_wait(height):
        size = layouts[height][1]
        part = pl.ds(pl.multiple_of((1 - core) * (size // 2), 16), size // 2)
        pltpu.make_async_remote_copy(
            src_ref=came[height].at[part],
            dst_ref=came[height].at[part],
            send_sem=relay_send.at[height],
            recv_sem=relay_recv.at[height],
            device_id=(partner(1),),
            device_id_type=MESH,
        ).wait_recv()

    routes = {1: (0, 1), 2: (0, 2), 4: (0, 4), 3: (2, 1), 5: (4, 1), 7: (6, 1)}

    def bulk(slot, q):
        if slot == 6:
            source, mask = (2, 4) if q < CHUNKS // 2 else (4, 2)
        else:
            source, mask = routes[slot]
        extent = pitch + (rhs // 2 if q == CHUNKS - 1 else 0)
        part = pl.ds(q * pitch, extent)
        return pltpu.make_async_remote_copy(
            src_ref=G.at[source, part],
            dst_ref=G.at[slot, part],
            send_sem=bulk_send.at[slot, q],
            recv_sem=bulk_recv.at[slot, q],
            device_id=(partner(mask),),
            device_id_type=MESH,
        )

    state = {}

    def lift(height, w):
        return mm(w, lifts[height] if height else t_ref[0, 0], PRECISE)

    state["w"], state["Z"], state["C"] = w, Z, {}
    state["partial"] = lift(0, w)
    write_message(0, w, Z, state["partial"], lifts)

    barrier = pltpu.get_barrier_semaphore()
    for bit in range(levels):
        pl.semaphore_signal(barrier, inc=1, device_id=(partner(1 << bit),), device_id_type=MESH)
    pl.semaphore_wait(barrier, levels)

    tree_copy(0).start()
    low_half, high_half = range(CHUNKS // 2), range(CHUNKS // 2, CHUNKS)
    for q, r in zip(low_half, high_half):
        bulk(2, q).start()
        bulk(4, r).start()
    for q in range(CHUNKS):
        bulk(1, q).start()

    acc[...] = jnp.zeros_like(acc)
    far_acc[...] = jnp.zeros_like(far_acc)
    for q in range(CHUNKS):
        own = x_ref[q * rows_each : (q + 1) * rows_each, :]
        own_norm = norm_column(own, scale)
        part = slice(q * rows_each, (q + 1) * rows_each)

        def own_tile(step, carry, own=own, own_norm=own_norm, part=part):
            at = pl.ds(pl.multiple_of(step * tile, tile), tile)
            block = gauss(own, own_norm, x_ref[at, :], norm_row[:, at], scale)
            acc[:, at] += contract_both(b_high[:, part], b_low[:, part], block)
            return carry

        lax.fori_loop(0, points // tile, own_tile, 0)

    def advance(height):
        rows = layouts[height][0]
        sibling_Z = came[height][0:rank, :]
        if height >= TOP:
            high, low = read_pair(height, "w")
            block = gauss(
                sibling_Z,
                norm_column(sibling_Z, scale),
                state["Z"],
                as_row(norm_column(state["Z"], scale)),
                scale,
            )
            state["C"][height] = contract_both(high, low, block)
        if height + 1 == levels:
            return
        high, low = read_pair(height, "p")
        state["w"] = state["partial"] + (high.astype(F32) + low.astype(F32))
        for upper in range(height + 1, levels - 1):
            high = get_folded(came[height], rows[upper], rank, rank)
            low = get_folded(came[height], rows[upper] + rank // 2, rank, rank)
            lifts[upper] = lifts[upper] + (high.astype(F32) + low.astype(F32))
        pick = picks(height + 1, me // (2 << height))
        shift = rank * ((me // (1 << height)) % 2)
        pick = jnp.where(pick >= shift, pick - shift, pick + shift)
        state["Z"] = (
            mm(one_hot(pick, rank, 0), state["Z"]) + mm(one_hot(pick, rank, rank), sibling_Z)
        ).astype(BF16)
        if height + 2 < levels:
            state["partial"] = lift(height + 1, state["w"])
        else:
            state["partial"] = None
        write_message(height + 1, state["w"], state["Z"], state["partial"], lifts)
        tree_copy(height + 1).start()

    tree_copy(0).wait_recv()
    advance(0)
    for q, r in zip(low_half, high_half):
        bulk(2, r).start()
        bulk(4, q).start()

    def arrive(slot, q):
        bulk(slot, q).wait_recv()
        if slot in (2, 4, 6):
            bulk(slot + 1, q).start()
        if (slot == 2 and q < CHUNKS // 2) or (slot == 4 and q >= CHUNKS // 2):
            bulk(6, q).start()

    def near(slot, q):
        at_row = q * pitch
        theirs = G[slot, at_row : at_row + rows_each, :]
        flag = jnp.where(slot > 0, 1.0, 0.0)
        start, half = at_row + rows_each, rhs // 2
        both = G[slot, start : start + rhs, :]
        high = jnp.concatenate([both[:half, :rows_each], both[:half, rows_each:]], 0)
        low = jnp.concatenate([both[half:, :rows_each], both[half:, rows_each:]], 0)
        high = (high.astype(F32) * flag).astype(BF16)
        low = (low.astype(F32) * flag).astype(BF16)
        their_norm = norm_column(theirs, scale)

        def one_tile(step, carry):
            at = pl.ds(pl.multiple_of(step * tile, tile), tile)
            block = gauss(theirs, their_norm, x_ref[at, :], norm_row[:, at], scale)
            acc[:, at] += contract_both(high, low, block)
            return carry

        lax.fori_loop(0, points // tile, one_tile, 0)

    def far(slot):
        pick = picks(0, partner(slot))
        rows = None
        for q in range(CHUNKS):
            term = mm(
                one_hot(pick, rows_each, q * rows_each),
                G[slot, q * pitch : q * pitch + rows_each, :],
            )
            rows = term if rows is None else rows + term
        rows = rows.astype(BF16)
        coeff = get_folded(G.at[slot], tail, rhs, rank)
        coeff = (coeff.astype(F32) * (1.0 - near_flag(slot))).astype(BF16)
        block = gauss(rows, norm_column(rows, scale), leaf_Z, leaf_Z_row, scale)
        far_acc[...] += contract(coeff, block)

    def first_half(height):
        tree_copy(height).wait_recv()
        relay_copy(height).start()

    def second_half(height):
        relay_wait(height)
        advance(height)

    tree_steps = []
    for height in range(1, levels):
        tree_steps.append(functools.partial(first_half, height))
        tree_steps.append(functools.partial(second_half, height))

    def tree_step():
        if tree_steps:
            tree_steps.pop(0)()

    for q in range(CHUNKS):
        arrive(1, q)
    far(1)
    orders = [(q, r) for q, r in zip(low_half, high_half)]
    orders += [(r, q) for q, r in zip(low_half, high_half)]
    for q, r in orders:
        arrive(2, q)
        arrive(4, r)
        tree_step()
        arrive(3, q)
        arrive(5, r)
        tree_step()
    for slot in (2, 4, 3, 5):
        far(slot)
        tree_step()
    for q, r in zip(low_half, high_half):
        arrive(6, q)
        arrive(6, r)
    while tree_steps:
        tree_step()

    down = state["C"][levels - 1]
    for height in range(levels - 2, -1, -1):
        down = mm_nt(down, lifts[height] if height else t_ref[0, 0], PRECISE)
        if height in state["C"]:
            down = down + state["C"][height]
    for q in range(CHUNKS):
        arrive(7, q)
    far(6)
    far(7)
    for slot in near_ids:
        for q in range(CHUNKS):
            near(slot, q)
    total = acc[...] + mm_nt(down + far_acc[...], v_ref[...], PRECISE)
    out_ref[...] = jnp.concatenate([total, jnp.zeros_like(total)], 0).T[:, :rhs]

    for slot in range(1, GROUP):
        for q in range(CHUNKS):
            bulk(slot, q).wait_send()
    for height in range(levels):
        tree_copy(height).wait_send()
        if height:
            relay_copy(height).wait_send()


def solution(mesh):
    leaves = mesh.shape["leaf"]
    levels = leaves.bit_length() - 1

    def per_device(points, weights, leaf_basis, transfer, skeleton_index, node_owner, near_list):
        count, embed = points.shape
        rhs, rank = weights.shape[1], leaf_basis.shape[1]
        pitch = count // CHUNKS + rhs
        vmem = pl.BlockSpec(memory_space=pltpu.VMEM)
        smem = pl.BlockSpec(memory_space=pltpu.SMEM)
        sizes = [message_rows(levels, rank, rhs, height)[1] for height in range(levels)]
        buffers = [pltpu.VMEM((size, embed), BF16) for size in sizes]
        return pl.pallas_call(
            functools.partial(kernel, levels, 2.0 / embed, min(512, count)),
            out_shape=jax.ShapeDtypeStruct((count, rhs), F32),
            in_specs=[vmem] * 5 + [smem] * 2,
            out_specs=vmem,
            scratch_shapes=[
                pltpu.VMEM((GROUP, CHUNKS * pitch + rhs // 2, embed), BF16),
                pltpu.VMEM((rhs, count), F32),
                pltpu.VMEM((rhs, rank), F32),
                pltpu.VMEM((1, count), F32),
                *buffers,
                *buffers,
                pltpu.SemaphoreType.DMA((GROUP, CHUNKS)),
                pltpu.SemaphoreType.DMA((GROUP, CHUNKS)),
                pltpu.SemaphoreType.DMA((levels,)),
                pltpu.SemaphoreType.DMA((levels,)),
                pltpu.SemaphoreType.DMA((levels,)),
                pltpu.SemaphoreType.DMA((levels,)),
            ],
            compiler_params=pltpu.CompilerParams(
                collective_id=0, has_side_effects=True, vmem_limit_bytes=52 * 2**20
            ),
        )(points, weights, leaf_basis, transfer, skeleton_index, node_owner, near_list)

    return jax.shard_map(
        per_device,
        mesh=mesh,
        in_specs=(
            P("leaf", None),
            P("leaf", None),
            P("leaf", None),
            P("leaf", None, None, None),
            P(),
            P(),
            P(),
        ),
        out_specs=P("leaf", None),
        check_vma=False,
    )
```
